32 devices in a mesh: rx: 4 (over x, core), ry: 8 (over z, y).
Axes of the slice: x: 2, y: 2, z: 4, core: 2. Of those that a mesh axis runs over, the one named last changes fastest.
Arguments:
- liquid_share: float32 [1024, 5, 640], P(('rx', 'ry')), may hold values from 0 to 1
- thermal_field: float32 [1024, 5, 640], P(('rx', 'ry')), may hold values from -6 to 6
- destination_slab_line: int32 [32, 8, 4], P(('rx', 'ry')), may hold values from 0 to 128, as said below
Outputs:
- image: float32 [4, 4, 32, 640], P(None, None, ('rx', 'ry'))
The draws below stay inside these ranges and needn't reach their ends.
Inputs may be any that keep to these rules, and one draw needn't show every extreme that they name: `destination_slab_line`: live rows named for one receiving device are distinct. In every draw, in each rx row, some receiving device gets a live brick in all 32 of its slots; the others get between 8 and 32 live bricks.
All inputs are finite; a program needn't handle non-finite values.
Results may differ from the reference program's by a relative error of at most 0.0003.
Values sent between devices are 32-bit elements; how exact they have to be, the bound alone decides.
A program may use at most 128 MiB of HBM per device.

```python
import jax
import jax.numpy as jnp
from jax import lax

LINE_CELLS = 640
SHEET_NUMBER = 5
ROWS_DEV = 4
CAP = 4
PARCEL_CAPACITY = 32
NZ = 160
N_RX = 4
N_RY = 8


def draw_destination_slab_line(key, part):
    key = jax.random.fold_in(key, 11)
    devices = N_RX * N_RY
    slot_count = N_RY * CAP
    rows_total = ROWS_DEV * devices
    device_keys = jax.random.split(key, devices)

    def one_device(device_key):
        first_key, second_key, third_key = jax.random.split(device_key, 3)
        chosen_rows = jax.random.permutation(first_key, rows_total)[:slot_count].astype(jnp.int32)
        slot_order = jax.random.permutation(second_key, slot_count).astype(jnp.int32)
        live_count = jax.random.randint(third_key, (), slot_count // 4, slot_count + 1, dtype=jnp.int32)
        masked = jnp.where(slot_order < live_count, chosen_rows, rows_total)
        return (chosen_rows, masked.astype(jnp.int32))
    full_rows, masked_rows = jax.vmap(one_device)(device_keys)
    picked = jax.random.randint(jax.random.fold_in(key, 5), (N_RX,), 0, N_RY, dtype=jnp.int32)
    device_ids = jnp.arange(devices, dtype=jnp.int32)
    full_device = device_ids % N_RY == picked[device_ids // N_RY]
    values = jnp.where(full_device[:, None], full_rows, masked_rows)
    return values.reshape(devices, N_RY, CAP).astype(jnp.int32)


def block_scale(stream_key, extent, pieces, least, largest):
    gain, own = 1.0, jax.random.fold_in(stream_key, 6)
    for dim, blocks in pieces:
        steps = jnp.exp(jax.random.uniform(jax.random.fold_in(own, dim), (blocks,), jnp.float32, least / len(pieces), largest / len(pieces)))
        gain = gain * jnp.repeat(steps, extent[dim] // blocks).reshape([-1 if axis == dim else 1 for axis in range(len(extent))])
    return gain


def centred(rng, extent, scale, most, cuts=(), kind=jnp.bfloat16):
    result = scale * jax.random.normal(rng, extent, jnp.float32)
    if cuts:
        result = result * block_scale(rng, extent, cuts, -0.22, 0.18)
    return jnp.clip(result, -most, most).astype(kind)


def setup_inputs(seed: int = 0) -> dict:
    key_list = jax.random.split(jax.random.key(seed), 4)
    return {
        "liquid_share": jnp.clip(1.0 * jax.random.uniform(key_list[0], (N_RX * N_RY * PARCEL_CAPACITY, SHEET_NUMBER, LINE_CELLS), jnp.float32) ** block_scale(key_list[0], (N_RX * N_RY * PARCEL_CAPACITY, SHEET_NUMBER, LINE_CELLS), ((0, 32),), -0.2, 0.2), 0.0, 1.0),
        "thermal_field": centred(key_list[1], (N_RX * N_RY * PARCEL_CAPACITY, SHEET_NUMBER, LINE_CELLS), 1.0, 6.0, ((0, 32),), jnp.float32),
        "destination_slab_line": draw_destination_slab_line(jax.random.fold_in(key_list[3], 71), 0),
    }


OPACITY = 12.0

def along_depth(field):
    return 0.25 * field[..., :-2, :, :] + 0.5 * field[..., 1:-1, :, :] + 0.25 * field[..., 2:, :, :]

def along_plane(field):
    leading = [(0, 0)] * (field.ndim - 2)
    padded = jnp.pad(field, leading + [(1, 1), (0, 0)])
    field = 0.25 * padded[..., :-2, :] + 0.5 * padded[..., 1:-1, :] + 0.25 * padded[..., 2:, :]
    padded = jnp.pad(field, leading + [(0, 0), (1, 1)])
    return 0.25 * padded[..., :-2] + 0.5 * padded[..., 1:-1] + 0.25 * padded[..., 2:]

def render_slab(melt_ext, temp_inner, total_depth):
    inner = melt_ext[1:-1]
    grad_z = 0.5 * (melt_ext[2:] - melt_ext[:-2])
    padded = jnp.pad(inner, ((0, 0), (1, 1), (0, 0)))
    grad_y = 0.5 * (padded[:, 2:, :] - padded[:, :-2, :])
    padded = jnp.pad(inner, ((0, 0), (0, 0), (1, 1)))
    grad_x = 0.5 * (padded[:, :, 2:] - padded[:, :, :-2])
    facing = (0.48 * grad_z + 0.6 * grad_y + 0.64 * grad_x) / jnp.sqrt(grad_z * grad_z + grad_y * grad_y + grad_x * grad_x + 0.01)
    shade = 0.3 + 0.7 * jnp.abs(facing)
    alpha = 1.0 - jnp.exp(inner * (-OPACITY / total_depth))
    through = jnp.cumprod(1.0 - alpha, axis=0)
    before = jnp.concatenate([jnp.ones_like(through[:1]), through[:-1]], axis=0)
    weight = before * alpha * shade
    red = lax.optimization_barrier(jnp.sum(weight * jax.nn.sigmoid(2.0 * temp_inner), axis=0))
    green = lax.optimization_barrier(jnp.sum(weight * jnp.exp(-temp_inner * temp_inner), axis=0))
    blue = lax.optimization_barrier(jnp.sum(weight * jax.nn.sigmoid(-2.0 * temp_inner), axis=0))
    return jnp.stack([red, green, blue, through[-1]])

def layer_over(front, back):
    return jnp.concatenate([front[:3] + front[3:] * back[:3], front[3:] * back[3:]], axis=0)

def reference(liquid_share, thermal_field, destination_slab_line):
    devices = N_RX * N_RY
    rows_total = ROWS_DEV * devices

    def reshuffle_parcels(field):
        field = field.reshape(N_RX, N_RY, N_RY, CAP, SHEET_NUMBER, LINE_CELLS)
        return jnp.transpose(field, (0, 2, 1, 3, 4, 5)).reshape(devices, N_RY * CAP, SHEET_NUMBER, LINE_CELLS)
    liquid_share_placed = reshuffle_parcels(liquid_share)
    thermal_field_placed = reshuffle_parcels(thermal_field)
    targets = destination_slab_line.reshape(devices, N_RY * CAP)

    def place(index):
        inside = jnp.logical_and(index >= 0, index < devices).astype(liquid_share.dtype)
        clamped_place = jnp.clip(index, 0, devices - 1)
        parcels_held = jnp.stack([liquid_share_placed[clamped_place], thermal_field_placed[clamped_place]])
        empty = jnp.zeros((2, SHEET_NUMBER, rows_total, LINE_CELLS), liquid_share.dtype)
        slab = empty.at[:, :, targets[clamped_place], :].set(jnp.transpose(parcels_held, (0, 2, 1, 3)), mode='drop')
        return slab * inside

    def step(image, index):
        extended = jnp.concatenate([place(index - 1)[:, -2:], place(index), place(index + 1)[:, :2]], axis=1)
        smooth = along_depth(extended)
        layer_mask = jnp.ones((SHEET_NUMBER + 2,), liquid_share.dtype)
        layer_mask = layer_mask.at[0].set(jnp.where(index == 0, 0.0, 1.0))
        layer_mask = layer_mask.at[SHEET_NUMBER + 1].set(jnp.where(index == devices - 1, 0.0, 1.0))
        smooth = along_plane(smooth * layer_mask[None, :, None, None])
        part = render_slab(smooth[0], smooth[1, 1:-1], NZ)
        return (layer_over(image, part), None)
    start = jnp.concatenate([jnp.zeros((3, rows_total, LINE_CELLS), liquid_share.dtype), jnp.ones((1, rows_total, LINE_CELLS), liquid_share.dtype)], axis=0)
    image = lax.scan(step, start, jnp.arange(devices, dtype=jnp.int32))[0]
    return image.reshape(4, ROWS_DEV, devices, LINE_CELLS)
```

```python
import functools

import jax
import jax.numpy as jnp
from jax import lax
from jax.experimental import pallas as pl
from jax.experimental.pallas import tpu as pltpu
from jax.sharding import PartitionSpec as P

ROWS_DEV = 4
OPACITY = 12.0
MESH = pl.DeviceIdType.MESH
F32 = jnp.float32
BF16 = jnp.bfloat16


def kernel(
    n_rx, n_ry, cap, layers, width,
    melt_ref, temp_ref, t_ref, out_ref,
    send, recv, before, after, lines,
    rhs_b, rhs_d, rhs_e, rhs_p, rhs_n, weights,
    sm, st, gy, gx, img, cin, send2, parts,
    a_send, a_recv, hp_send, hp_recv, hn_send, hn_recv, t_send, t_recv,
    c_send, c_recv, d_send, d_recv,
):
    n_dev = n_rx * n_ry
    rows = ROWS_DEV * n_dev
    half_rows = rows // 2
    n_low = n_dev // 2
    k0 = n_ry * 2 * cap
    r, j = lax.axis_index("rx"), lax.axis_index("ry")
    me = r * n_ry + j
    core = r % 2

    def worker(rr, dd):
        return ((rr // 2) * 2 + dd % 2, (dd // 2) * 2 + rr % 2)

    def worker_of(slab):
        return worker(slab // n_ry, slab % n_ry)

    src_r, slab_d = worker(r, j)
    slab = src_r * n_ry + slab_d
    own_block = core == j % 2
    has_prev, has_next = slab > 0, slab < n_dev - 1

    barrier = pltpu.get_barrier_semaphore()

    def greet(i, c):
        other = (me + i) % n_dev
        pl.semaphore_signal(barrier, inc=1, device_id=(other // n_ry, other % n_ry), device_id_type=MESH)
        return c

    lax.fori_loop(1, n_dev, greet, 0)

    for field, ref in enumerate((melt_ref, temp_ref)):
        for b in range(n_ry * cap):
            d = b // cap
            send[d * layers : (d + 1) * layers, field * cap + b % cap, :] = ref[b]

    @pl.when(jnp.logical_not(has_prev))
    def _():
        before[...] = jnp.zeros_like(before)
        lines[1] = jnp.full_like(lines[1], 1e4)

    @pl.when(jnp.logical_not(has_next))
    def _():
        after[...] = jnp.zeros_like(after)
        lines[2] = jnp.full_like(lines[2], 1e4)

    pl.semaphore_wait(barrier, n_dev - 1)

    def line_copy(which, target):
        return pltpu.make_async_remote_copy(
            t_ref, lines.at[which], t_send.at[which], t_recv.at[which],
            device_id=target, device_id_type=MESH)

    @pl.when(me < n_dev - 1)
    def _():
        line_copy(1, worker_of(me + 1)).start()

    @pl.when(me > 0)
    def _():
        line_copy(2, worker_of(me - 1)).start()

    @pl.when(own_block)
    def _():
        lines[0] = t_ref[...]

    @pl.when(jnp.logical_not(own_block))
    def _():
        line_copy(0, worker(r, j)).start()

    def brick_copy(i):
        d = (j + i) % n_ry
        return pltpu.make_async_remote_copy(
            send.at[pl.ds(d * layers, layers)], recv.at[j], a_send.at[i], a_recv.at[j],
            device_id=worker(r, d), device_id_type=MESH)

    for i in range(1, n_ry):
        brick_copy(i).start()

    @pl.when(jnp.logical_not(own_block))
    def _():
        brick_copy(0).start()

    @pl.when(own_block)
    def _():
        recv[j] = send[pl.ds(j * layers, layers)]

    @pl.when(jnp.logical_not(own_block))
    def _():
        line_copy(0, worker(r, j)).wait_recv()

    @pl.when(has_prev)
    def _():
        line_copy(1, worker(r, j)).wait_recv()

    @pl.when(has_next)
    def _():
        line_copy(2, worker(r, j)).wait_recv()

    p = lax.broadcasted_iota(jnp.int32, (rows, 2 * k0), 0)
    lane = lax.broadcasted_iota(jnp.int32, (rows, 2 * k0), 1)
    log_ry, log_low = n_ry.bit_length() - 1, n_low.bit_length() - 1
    other_half = jnp.where(p < half_rows, 1, 0)
    side = jnp.where(other_half == 1, 1 - core, core)
    part_a = (p >> log_low) & (ROWS_DEV - 1)
    low = p & (n_low - 1)
    k = ((low >> log_ry) << (log_ry + 1)) + side * n_ry + (low & (n_ry - 1))
    q = (part_a * n_dev + k).astype(F32)
    is_melt = (lane & cap) == 0

    def hat(v):
        return jnp.maximum(0.5 - 0.25 * jnp.abs(v), 0.0)

    for which in range(3):
        u = lines[which, 0:1, :] - q
        s = hat(u)
        g = 0.5 * (jnp.where(q < rows - 1, hat(u - 1.0), 0.0) - jnp.where(q > 0, hat(u + 1.0), 0.0))
        weights[which, 0:rows] = jnp.where(is_melt, s, 0.0).astype(BF16)
        weights[which, rows : 2 * rows] = jnp.where(is_melt, 0.0, s).astype(BF16)
        weights[which, 2 * rows : 3 * rows] = jnp.where(is_melt, g, 0.0).astype(BF16)

    col = lax.broadcasted_iota(jnp.int32, (4 * cap, width), 1)

    def from_left(x):
        return jnp.where(col == 0, 0.0, pltpu.roll(x, 1, 1))

    def from_right(x):
        return jnp.where(col == width - 1, 0.0, pltpu.roll(x, width - 1, 1))

    def smooth_x(x):
        return 0.5 * x + 0.25 * (from_left(x) + from_right(x))

    def diff_x(x):
        return 0.5 * (from_right(x) - from_left(x))

    def put(ref, index, first, x):
        hi = x.astype(BF16)
        ref[index, first : first + 4 * cap] = hi
        ref[index, k0 + first : k0 + first + 4 * cap] = (x - hi.astype(F32)).astype(BF16)

    def rows_of(ref, pair, layer):
        return ref[2 * pair : 2 * pair + 2, layer].reshape(4 * cap, width)

    def before_copy(jj):
        return pltpu.make_async_remote_copy(
            recv.at[jj, pl.ds(layers - 2, 2)], before.at[jj], hp_send.at[jj], hp_recv.at[jj],
            device_id=worker_of((slab + 1) % n_dev), device_id_type=MESH)

    def after_copy(jj):
        return pltpu.make_async_remote_copy(
            recv.at[jj, pl.ds(0, 2)], after.at[jj], hn_send.at[jj], hn_recv.at[jj],
            device_id=worker_of((slab + n_dev - 1) % n_dev), device_id_type=MESH)

    def brick_wait(jj):
        pltpu.make_async_remote_copy(
            send.at[pl.ds(0, layers)], recv.at[jj], a_send.at[0], a_recv.at[jj],
            device_id=worker(r, j), device_id_type=MESH).wait_recv()

    for pair in range(n_ry // 2):
        for jj in (2 * pair, 2 * pair + 1):
            @pl.when(jnp.logical_not(jnp.logical_and(own_block, j == jj)))
            def _():
                brick_wait(jj)

            @pl.when(has_next)
            def _():
                before_copy(jj).start()

            @pl.when(has_prev)
            def _():
                after_copy(jj).start()

        first = pair * 4 * cap
        xs = [smooth_x(rows_of(recv, pair, z)) for z in range(layers)]
        for z in range(layers):
            b = 0.5 * xs[z]
            if z > 0:
                b = b + 0.25 * xs[z - 1]
            if z < layers - 1:
                b = b + 0.25 * xs[z + 1]
            put(rhs_b, z, first, b)
            put(rhs_d, z, first, diff_x(b))
        put(rhs_e, 0, first, 0.25 * xs[0])
        put(rhs_e, 1, first, 0.25 * xs[layers - 1])

    def dot(which, lo, hi, rhs):
        return jnp.dot(weights[which, lo * rows : hi * rows], rhs, preferred_element_type=F32)

    for z in range(layers):
        res = dot(0, 0, 3, rhs_b[z])
        sm[z + 1] = res[0:rows]
        st[z] = res[rows : 2 * rows]
        gy[z] = res[2 * rows : 3 * rows]
        gx[z] = dot(0, 0, 1, rhs_d[z])
    sm[0] = dot(0, 0, 1, rhs_e[0])
    sm[layers + 1] = dot(0, 0, 1, rhs_e[1])

    for pair in range(n_ry // 2):
        for jj in (2 * pair, 2 * pair + 1):
            @pl.when(has_prev)
            def _():
                before_copy(jj).wait_recv()

            @pl.when(has_next)
            def _():
                after_copy(jj).wait_recv()

        first = pair * 4 * cap
        p3, p4 = (smooth_x(rows_of(before, pair, z)) for z in (0, 1))
        n0, n1 = (smooth_x(rows_of(after, pair, z)) for z in (0, 1))
        put(rhs_p, 0, first, 0.25 * p4)
        put(rhs_p, 1, first, 0.25 * diff_x(p4))
        put(rhs_p, 2, first, 0.25 * p3 + 0.5 * p4)
        put(rhs_n, 0, first, 0.25 * n0)
        put(rhs_n, 1, first, 0.25 * diff_x(n0))
        put(rhs_n, 2, first, 0.25 * n1 + 0.5 * n0)

    for which, rhs, z, edge, present in ((1, rhs_p, 0, 0, has_prev), (2, rhs_n, layers - 1, layers + 1, has_next)):
        res = dot(which, 0, 3, rhs[0])
        sm[z + 1] += res[0:rows]
        st[z] += res[rows : 2 * rows]
        gy[z] += res[2 * rows : 3 * rows]
        gx[z] += dot(which, 0, 1, rhs[1])
        sm[edge] = jnp.where(present, sm[edge] + dot(which, 0, 1, rhs[2]), 0.0)

    decay = -OPACITY / (layers * n_dev)

    def march(half):
        def tile(i, c):
            at = pl.ds(pl.multiple_of(half * half_rows + i * 8, 8), 8)
            through = total = red = green = None
            for z in range(layers):
                s = sm[z + 1, at, :]
                dz = 0.5 * (sm[z + 2, at, :] - sm[z, at, :])
                dy, dx = gy[z, at, :], gx[z, at, :]
                t = st[z, at, :]
                facing = (0.48 * dz + 0.6 * dy + 0.64 * dx) * lax.rsqrt(dz * dz + dy * dy + dx * dx + 0.01)
                shade = 0.3 + 0.7 * jnp.abs(facing)
                kept = jnp.exp(s * decay)
                w = (1.0 - kept) * shade
                if z > 0:
                    w = w * through
                rw = w / (1.0 + jnp.exp(-2.0 * t))
                gw = w * jnp.exp(-t * t)
                if z == 0:
                    through, total, red, green = kept, w, rw, gw
                else:
                    through, total, red, green = through * kept, total + w, red + rw, green + gw
            to = pl.ds(pl.multiple_of(i * 8, 8), 8)
            img[half, 0, to, :] = red
            img[half, 1, to, :] = green
            img[half, 2, to, :] = total - red
            img[half, 3, to, :] = through
            return c

        lax.fori_loop(0, half_rows // 8, tile, 0)

    march(0)
    core_copy = pltpu.make_async_remote_copy(
        img.at[0], cin, c_send, c_recv, device_id=((r // 2) * 2 + 1 - core, j), device_id_type=MESH)
    core_copy.start()
    march(1)
    core_copy.wait_recv()

    front = core == 0

    for a in range(ROWS_DEV):
        for low8 in range(n_low // 8):
            at = slice(a * n_low + low8 * 8, a * n_low + low8 * 8 + 8)
            mine = [img[1, ch, at, :] for ch in range(4)]
            theirs = [cin[ch, at, :] for ch in range(4)]
            ft = jnp.where(front, mine[3], theirs[3])
            for ch in range(4):
                f = jnp.where(front, mine[ch], theirs[ch])
                b = jnp.where(front, theirs[ch], mine[ch])
                value = f + ft * b if ch < 3 else ft * b
                send2[low8 * 8 : low8 * 8 + 8, ch * ROWS_DEV + a, :] = value

    low_me = (r // 2) * n_ry + j
    group = (r // 2) * n_ry + (j % 2) * (n_ry // 2) + j // 2

    def part_copy(i):
        to = (low_me + i) % n_low
        return pltpu.make_async_remote_copy(
            send2.at[to], parts.at[group], d_send.at[i], d_recv.at[group],
            device_id=((to // n_ry) * 2 + core, to % n_ry), device_id_type=MESH)

    for i in range(1, n_low):
        part_copy(i).start()
    parts[group] = send2[low_me]

    color, through = None, None
    for g in range(n_low):
        @pl.when(g != group)
        def _():
            pltpu.make_async_remote_copy(
                send2.at[0], parts.at[g], d_send.at[0], d_recv.at[g],
                device_id=(r, j), device_id_type=MESH).wait_recv()

        value = parts[g]
        c = value[: 3 * ROWS_DEV]
        t = value[3 * ROWS_DEV :]
        if g == 0:
            color, through = c, t
        else:
            color = color + jnp.concatenate([through] * 3, axis=0) * c
            through = through * t
    out_ref[: 3 * ROWS_DEV] = color
    out_ref[3 * ROWS_DEV :] = through

    @pl.when(me < n_dev - 1)
    def _():
        line_copy(1, worker(r, j)).wait_send()

    @pl.when(me > 0)
    def _():
        line_copy(2, worker(r, j)).wait_send()

    @pl.when(jnp.logical_not(own_block))
    def _():
        line_copy(0, worker(r, j)).wait_send()
        brick_copy(0).wait_send()

    for i in range(1, n_ry):
        brick_copy(i).wait_send()
    for jj in range(n_ry):
        @pl.when(has_next)
        def _():
            before_copy(jj).wait_send()

        @pl.when(has_prev)
        def _():
            after_copy(jj).wait_send()

    core_copy.wait_send()
    for i in range(1, n_low):
        part_copy(i).wait_send()


def shards(liquid_share, thermal_field, destination_slab_line):
    n_rx, n_ry = lax.axis_size("rx"), lax.axis_size("ry")
    bricks, layers, width = liquid_share.shape
    cap = bricks // n_ry
    n_dev = n_rx * n_ry
    rows = ROWS_DEV * n_dev
    k0 = n_ry * 2 * cap
    lines = destination_slab_line.reshape(n_ry, 1, cap).astype(F32)
    lines = jnp.where(lines >= rows, 1e4, lines)
    lines = jnp.broadcast_to(lines, (n_ry, 2, cap)).reshape(1, k0)
    lines = jnp.broadcast_to(jnp.concatenate([lines, lines], axis=1), (8, 2 * k0))
    dma = pltpu.SemaphoreType.DMA
    vmem = pltpu.VMEM
    half_rows, n_low = rows // 2, n_dev // 2
    image = pl.pallas_call(
        functools.partial(kernel, n_rx, n_ry, cap, layers, width),
        out_shape=jax.ShapeDtypeStruct((4 * ROWS_DEV, width), F32),
        in_specs=[pl.BlockSpec(memory_space=pltpu.VMEM)] * 3,
        out_specs=pl.BlockSpec(memory_space=pltpu.VMEM),
        scratch_shapes=[
            vmem((n_ry * layers, 2 * cap, width), F32),
            vmem((n_ry, layers, 2 * cap, width), F32),
            vmem((n_ry, 2, 2 * cap, width), F32),
            vmem((n_ry, 2, 2 * cap, width), F32),
            vmem((3, 8, 2 * k0), F32),
            vmem((layers, 2 * k0, width), BF16),
            vmem((layers, 2 * k0, width), BF16),
            vmem((2, 2 * k0, width), BF16),
            vmem((3, 2 * k0, width), BF16),
            vmem((3, 2 * k0, width), BF16),
            vmem((3, 3 * rows, 2 * k0), BF16),
            vmem((layers + 2, rows, width), F32),
            vmem((layers, rows, width), F32),
            vmem((layers, rows, width), F32),
            vmem((layers, rows, width), F32),
            vmem((2, 4, half_rows, width), F32),
            vmem((4, half_rows, width), F32),
            vmem((n_low, 4 * ROWS_DEV, width), F32),
            vmem((n_low, 4 * ROWS_DEV, width), F32),
            dma((n_ry,)), dma((n_ry,)),
            dma((n_ry,)), dma((n_ry,)),
            dma((n_ry,)), dma((n_ry,)),
            dma((3,)), dma((3,)),
            dma, dma,
            dma((n_low,)), dma((n_low,)),
        ],
        compiler_params=pltpu.CompilerParams(
            collective_id=0, has_side_effects=True, vmem_limit_bytes=60 * 1024 * 1024),
    )(liquid_share, thermal_field, lines)
    return image.reshape(4, ROWS_DEV, 1, width)


def solution(mesh):
    return jax.shard_map(
        shards,
        mesh=mesh,
        in_specs=(
            P(("rx", "ry"), None, None),
            P(("rx", "ry"), None, None),
            P(("rx", "ry"), None, None),
        ),
        out_specs=P(None, None, ("rx", "ry"), None),
        check_vma=False,
    )
```

```python
import functools

import jax
import jax.numpy as jnp
from jax import lax
from jax.experimental import pallas as pl
from jax.experimental.pallas import tpu as pltpu
from jax.sharding import PartitionSpec as P

ROWS_DEV = 4
OPACITY = 12.0
MESH = pl.DeviceIdType.MESH
F32 = jnp.float32
BF16 = jnp.bfloat16


def kernel(
    n_rx, n_ry, cap, layers, width,
    melt_ref, temp_ref, names_ref, out_ref,
    held, t_ref, send, recv, before, after, lines,
    rhs_b, rhs_d, rhs_e, rhs_p, rhs_n, weights,
    sm, st, gy, gx, img, cin, send2, parts,
    a_send, a_recv, hp_send, hp_recv, hn_send, hn_recv, t_send, t_recv,
    c_send, c_recv, d_send, d_recv, in_sem,
):
    n_dev = n_rx * n_ry
    rows = ROWS_DEV * n_dev
    half_rows = rows // 2
    n_low = n_dev // 2
    k0 = n_ry * 2 * cap
    r, j = lax.axis_index("rx"), lax.axis_index("ry")
    me = r * n_ry + j
    core = r % 2

    def worker(rr, dd):
        return ((rr // 2) * 2 + dd % 2, (dd // 2) * 2 + rr % 2)

    def worker_of(slab):
        return worker(slab // n_ry, slab % n_ry)

    src_r, slab_d = worker(r, j)
    slab = src_r * n_ry + slab_d
    own_block = core == j % 2
    has_prev, has_next = slab > 0, slab < n_dev - 1

    barrier = pltpu.get_barrier_semaphore()

    def greet(i, c):
        other = (me + i) % n_dev
        pl.semaphore_signal(barrier, inc=1, device_id=(other // n_ry, other % n_ry), device_id_type=MESH)
        return c

    lax.fori_loop(1, n_dev, greet, 0)

    loads = [pltpu.make_async_copy(ref, held.at[i], in_sem.at[i]) for i, ref in enumerate((melt_ref, temp_ref))]
    for load in loads:
        load.start()

    lane8 = lax.broadcasted_iota(jnp.int32, (cap, 2 * k0), 1)
    row8 = lax.broadcasted_iota(jnp.int32, (cap, 2 * k0), 0)
    slot = (lane8 // (2 * cap)) & (n_ry - 1)
    named = names_ref[...].astype(F32)
    spread = jnp.zeros((cap, 2 * k0), F32)
    for jj in range(n_ry):
        spread = jnp.where(slot == (j + n_ry - jj) % n_ry, named[:, jj : jj + 1], spread)
    line = jnp.sum(jnp.where(row8 == (lane8 & (cap - 1)), spread, 0.0), axis=0, keepdims=True)
    line = jnp.where(line >= rows, 1e4, line)
    t_ref[...] = jnp.broadcast_to(line, (8, 2 * k0))

    for field in range(2):
        loads[field].wait()
        for d in range(n_ry):
            send[d * layers : (d + 1) * layers, field * cap : (field + 1) * cap, :] = (
                held[field, :, d * cap : (d + 1) * cap, :])

    @pl.when(jnp.logical_not(has_prev))
    def _():
        before[...] = jnp.zeros_like(before)
        lines[1] = jnp.full_like(lines[1], 1e4)

    @pl.when(jnp.logical_not(has_next))
    def _():
        after[...] = jnp.zeros_like(after)
        lines[2] = jnp.full_like(lines[2], 1e4)

    pl.semaphore_wait(barrier, n_dev - 1)

    def line_copy(which, target):
        return pltpu.make_async_remote_copy(
            t_ref, lines.at[which], t_send.at[which], t_recv.at[which],
            device_id=target, device_id_type=MESH)

    @pl.when(me < n_dev - 1)
    def _():
        line_copy(1, worker_of(me + 1)).start()

    @pl.when(me > 0)
    def _():
        line_copy(2, worker_of(me - 1)).start()

    @pl.when(own_block)
    def _():
        lines[0] = t_ref[...]

    @pl.when(jnp.logical_not(own_block))
    def _():
        line_copy(0, worker(r, j)).start()

    def brick_copy(i):
        d = (j + i) % n_ry
        return pltpu.make_async_remote_copy(
            send.at[pl.ds(d * layers, layers)], recv.at[i], a_send.at[i], a_recv.at[i],
            device_id=worker(r, d), device_id_type=MESH)

    for i in range(1, n_ry):
        brick_copy(i).start()

    @pl.when(jnp.logical_not(own_block))
    def _():
        brick_copy(0).start()

    @pl.when(own_block)
    def _():
        recv[0] = send[pl.ds(j * layers, layers)]

    @pl.when(jnp.logical_not(own_block))
    def _():
        line_copy(0, worker(r, j)).wait_recv()

    @pl.when(has_prev)
    def _():
        line_copy(1, worker(r, j)).wait_recv()

    @pl.when(has_next)
    def _():
        line_copy(2, worker(r, j)).wait_recv()

    p = lax.broadcasted_iota(jnp.int32, (rows, 2 * k0), 0)
    lane = lax.broadcasted_iota(jnp.int32, (rows, 2 * k0), 1)
    log_ry, log_low = n_ry.bit_length() - 1, n_low.bit_length() - 1
    other_half = jnp.where(p < half_rows, 1, 0)
    side = jnp.where(other_half == 1, 1 - core, core)
    part_a = (p >> log_low) & (ROWS_DEV - 1)
    low = p & (n_low - 1)
    k = ((low >> log_ry) << (log_ry + 1)) + side * n_ry + (low & (n_ry - 1))
    q = (part_a * n_dev + k).astype(F32)
    is_melt = (lane & cap) == 0

    def hat(v):
        return jnp.maximum(0.5 - 0.25 * jnp.abs(v), 0.0)

    for which in range(3):
        u = lines[which, 0:1, :] - q
        s = hat(u)
        g = 0.5 * (jnp.where(q < rows - 1, hat(u - 1.0), 0.0) - jnp.where(q > 0, hat(u + 1.0), 0.0))
        weights[which, 0:rows] = jnp.where(is_melt, s, 0.0).astype(BF16)
        weights[which, rows : 2 * rows] = jnp.where(is_melt, 0.0, s).astype(BF16)
        weights[which, 2 * rows : 3 * rows] = jnp.where(is_melt, g, 0.0).astype(BF16)

    col = lax.broadcasted_iota(jnp.int32, (4 * cap, width), 1)

    def from_left(x):
        return jnp.where(col == 0, 0.0, pltpu.roll(x, 1, 1))

    def from_right(x):
        return jnp.where(col == width - 1, 0.0, pltpu.roll(x, width - 1, 1))

    def smooth_x(x):
        return 0.5 * x + 0.25 * (from_left(x) + from_right(x))

    def diff_x(x):
        return 0.5 * (from_right(x) - from_left(x))

    def put(ref, index, first, x):
        hi = x.astype(BF16)
        ref[index, first : first + 4 * cap] = hi
        ref[index, k0 + first : k0 + first + 4 * cap] = (x - hi.astype(F32)).astype(BF16)

    def rows_of(ref, pair, layer):
        return ref[2 * pair : 2 * pair + 2, layer].reshape(4 * cap, width)

    def before_copy(jj):
        return pltpu.make_async_remote_copy(
            recv.at[jj, pl.ds(layers - 2, 2)], before.at[jj], hp_send.at[jj], hp_recv.at[jj],
            device_id=worker_of((slab + 1) % n_dev), device_id_type=MESH)

    def after_copy(jj):
        return pltpu.make_async_remote_copy(
            recv.at[jj, pl.ds(0, 2)], after.at[jj], hn_send.at[jj], hn_recv.at[jj],
            device_id=worker_of((slab + n_dev - 1) % n_dev), device_id_type=MESH)

    def brick_wait(jj):
        pltpu.make_async_remote_copy(
            send.at[pl.ds(0, layers)], recv.at[jj], a_send.at[0], a_recv.at[jj],
            device_id=worker(r, j), device_id_type=MESH).wait_recv()

    for pair in range(n_ry // 2):
        for jj in (2 * pair, 2 * pair + 1):
            if jj:
                brick_wait(jj)
            else:
                @pl.when(jnp.logical_not(own_block))
                def _():
                    brick_wait(0)

            @pl.when(has_next)
            def _():
                before_copy(jj).start()

            @pl.when(has_prev)
            def _():
                after_copy(jj).start()

        first = pair * 4 * cap
        xs = [smooth_x(rows_of(recv, pair, z)) for z in range(layers)]
        for z in range(layers):
            b = 0.5 * xs[z]
            if z > 0:
                b = b + 0.25 * xs[z - 1]
            if z < layers - 1:
                b = b + 0.25 * xs[z + 1]
            put(rhs_b, z, first, b)
            put(rhs_d, z, first, diff_x(b))
        put(rhs_e, 0, first, 0.25 * xs[0])
        put(rhs_e, 1, first, 0.25 * xs[layers - 1])

    def dot(which, lo, hi, rhs):
        return jnp.dot(weights[which, lo * rows : hi * rows], rhs, preferred_element_type=F32)

    for z in range(layers):
        res = dot(0, 0, 3, rhs_b[z])
        sm[z + 1] = res[0:rows]
        st[z] = res[rows : 2 * rows]
        gy[z] = res[2 * rows : 3 * rows]
        gx[z] = dot(0, 0, 1, rhs_d[z])
    sm[0] = dot(0, 0, 1, rhs_e[0])
    sm[layers + 1] = dot(0, 0, 1, rhs_e[1])

    for pair in range(n_ry // 2):
        for jj in (2 * pair, 2 * pair + 1):
            @pl.when(has_prev)
            def _():
                before_copy(jj).wait_recv()

            @pl.when(has_next)
            def _():
                after_copy(jj).wait_recv()

        first = pair * 4 * cap
        p3, p4 = (smooth_x(rows_of(before, pair, z)) for z in (0, 1))
        n0, n1 = (smooth_x(rows_of(after, pair, z)) for z in (0, 1))
        put(rhs_p, 0, first, 0.25 * p4)
        put(rhs_p, 1, first, 0.25 * diff_x(p4))
        put(rhs_p, 2, first, 0.25 * p3 + 0.5 * p4)
        put(rhs_n, 0, first, 0.25 * n0)
        put(rhs_n, 1, first, 0.25 * diff_x(n0))
        put(rhs_n, 2, first, 0.25 * n1 + 0.5 * n0)

    for which, rhs, z, edge, present in ((1, rhs_p, 0, 0, has_prev), (2, rhs_n, layers - 1, layers + 1, has_next)):
        res = dot(which, 0, 3, rhs[0])
        sm[z + 1] += res[0:rows]
        st[z] += res[rows : 2 * rows]
        gy[z] += res[2 * rows : 3 * rows]
        gx[z] += dot(which, 0, 1, rhs[1])
        sm[edge] = jnp.where(present, sm[edge] + dot(which, 0, 1, rhs[2]), 0.0)

    decay = -OPACITY / (layers * n_dev)

    quarter = half_rows // 2

    def march(half, part):
        def tile(i, c):
            at = pl.ds(pl.multiple_of(half * half_rows + part * quarter + i * 8, 8), 8)
            through = total = red = green = None
            for z in range(layers):
                s = sm[z + 1, at, :]
                dz = 0.5 * (sm[z + 2, at, :] - sm[z, at, :])
                dy, dx = gy[z, at, :], gx[z, at, :]
                t = st[z, at, :]
                facing = (0.48 * dz + 0.6 * dy + 0.64 * dx) * lax.rsqrt(dz * dz + dy * dy + dx * dx + 0.01)
                shade = 0.3 + 0.7 * jnp.abs(facing)
                kept = jnp.exp(s * decay)
                w = (1.0 - kept) * shade
                if z > 0:
                    w = w * through
                rw = w / (1.0 + jnp.exp(-2.0 * t))
                gw = w * jnp.exp(-t * t)
                if z == 0:
                    through, total, red, green = kept, w, rw, gw
                else:
                    through, total, red, green = through * kept, total + w, red + rw, green + gw
            to = pl.ds(pl.multiple_of(i * 8, 8), 8)
            img[half, part, 0, to, :] = red
            img[half, part, 1, to, :] = green
            img[half, part, 2, to, :] = total - red
            img[half, part, 3, to, :] = through
            return c

        lax.fori_loop(0, quarter // 8, tile, 0)

    def core_copy(part):
        return pltpu.make_async_remote_copy(
            img.at[0, part], cin.at[part], c_send.at[part], c_recv.at[part],
            device_id=((r // 2) * 2 + 1 - core, j), device_id_type=MESH)

    front = core == 0
    low_me = (r // 2) * n_ry + j
    group = (r // 2) * n_ry + (j % 2) * (n_ry // 2) + j // 2

    def part_copy(part, i):
        to = (low_me + i) % n_low
        return pltpu.make_async_remote_copy(
            send2.at[part, to], parts.at[part, group], d_send.at[part, i], d_recv.at[part, group],
            device_id=((to // n_ry) * 2 + core, to % n_ry), device_id_type=MESH)

    for part in range(2):
        march(0, part)
        core_copy(part).start()
        march(1, part)
        core_copy(part).wait_recv()
        for a in range(2):
            for low8 in range(n_low // 8):
                at = slice(a * n_low + low8 * 8, a * n_low + low8 * 8 + 8)
                mine = [img[1, part, ch, at, :] for ch in range(4)]
                theirs = [cin[part, ch, at, :] for ch in range(4)]
                ft = jnp.where(front, mine[3], theirs[3])
                for ch in range(4):
                    f = jnp.where(front, mine[ch], theirs[ch])
                    b = jnp.where(front, theirs[ch], mine[ch])
                    value = f + ft * b if ch < 3 else ft * b
                    send2[part, low8 * 8 : low8 * 8 + 8, ch * 2 + a, :] = value
        for i in range(1, n_low):
            part_copy(part, i).start()
        parts[part, group] = send2[part, low_me]

    for part in range(2):
        color, through = None, None
        for g in range(n_low):
            @pl.when(g != group)
            def _():
                pltpu.make_async_remote_copy(
                    send2.at[part, 0], parts.at[part, g], d_send.at[part, 0], d_recv.at[part, g],
                    device_id=(r, j), device_id_type=MESH).wait_recv()

            value = parts[part, g]
            t = jnp.concatenate([value[6:8]] * 4, axis=0)
            if g == 0:
                color, through = value, t
            else:
                color = color + through * value
                through = through * t
        for a in range(2):
            for ch in range(4):
                at = ch * 2 + a
                out_ref[ch, part * 2 + a] = (color if ch < 3 else through)[at : at + 1]

    @pl.when(me < n_dev - 1)
    def _():
        line_copy(1, worker(r, j)).wait_send()

    @pl.when(me > 0)
    def _():
        line_copy(2, worker(r, j)).wait_send()

    @pl.when(jnp.logical_not(own_block))
    def _():
        line_copy(0, worker(r, j)).wait_send()
        brick_copy(0).wait_send()

    for i in range(1, n_ry):
        brick_copy(i).wait_send()
    for jj in range(n_ry):
        @pl.when(has_next)
        def _():
            before_copy(jj).wait_send()

        @pl.when(has_prev)
        def _():
            after_copy(jj).wait_send()

    for part in range(2):
        core_copy(part).wait_send()
        for i in range(1, n_low):
            part_copy(part, i).wait_send()


def shards(liquid_share, thermal_field, destination_slab_line):
    n_rx, n_ry = lax.axis_size("rx"), lax.axis_size("ry")
    bricks, layers, width = liquid_share.shape
    cap = bricks // n_ry
    n_dev = n_rx * n_ry
    rows = ROWS_DEV * n_dev
    k0 = n_ry * 2 * cap
    dma = pltpu.SemaphoreType.DMA
    vmem = pltpu.VMEM
    half_rows, n_low = rows // 2, n_dev // 2
    image = pl.pallas_call(
        functools.partial(kernel, n_rx, n_ry, cap, layers, width),
        out_shape=jax.ShapeDtypeStruct((4, ROWS_DEV, 1, width), F32),
        in_specs=[pl.BlockSpec(memory_space=pl.ANY)] * 2 + [pl.BlockSpec(memory_space=pltpu.VMEM)],
        out_specs=pl.BlockSpec(memory_space=pltpu.VMEM),
        scratch_shapes=[
            vmem((2, layers, bricks, width), F32),
            vmem((8, 2 * k0), F32),
            vmem((n_ry * layers, 2 * cap, width), F32),
            vmem((n_ry, layers, 2 * cap, width), F32),
            vmem((n_ry, 2, 2 * cap, width), F32),
            vmem((n_ry, 2, 2 * cap, width), F32),
            vmem((3, 8, 2 * k0), F32),
            vmem((layers, 2 * k0, width), BF16),
            vmem((layers, 2 * k0, width), BF16),
            vmem((2, 2 * k0, width), BF16),
            vmem((3, 2 * k0, width), BF16),
            vmem((3, 2 * k0, width), BF16),
            vmem((3, 3 * rows, 2 * k0), BF16),
            vmem((layers + 2, rows, width), F32),
            vmem((layers, rows, width), F32),
            vmem((layers, rows, width), F32),
            vmem((layers, rows, width), F32),
            vmem((2, 2, 4, half_rows // 2, width), F32),
            vmem((2, 4, half_rows // 2, width), F32),
            vmem((2, n_low, 2 * ROWS_DEV, width), F32),
            vmem((2, n_low, 2 * ROWS_DEV, width), F32),
            dma((n_ry,)), dma((n_ry,)),
            dma((n_ry,)), dma((n_ry,)),
            dma((n_ry,)), dma((n_ry,)),
            dma((3,)), dma((3,)),
            dma((2,)), dma((2,)),
            dma((2, n_low)), dma((2, n_low)),
            dma((2,)),
        ],
        compiler_params=pltpu.CompilerParams(
            collective_id=0, has_side_effects=True, vmem_limit_bytes=60 * 1024 * 1024),
    )(
        jnp.transpose(liquid_share, (1, 0, 2)),
        jnp.transpose(thermal_field, (1, 0, 2)),
        jnp.transpose(destination_slab_line[0]),
    )
    return image


def solution(mesh):
    return jax.shard_map(
        shards,
        mesh=mesh,
        in_specs=(
            P(("rx", "ry"), None, None),
            P(("rx", "ry"), None, None),
            P(("rx", "ry"), None, None),
        ),
        out_specs=P(None, None, ("rx", "ry"), None),
        check_vma=False,
    )
```

```python
import functools

import jax
import jax.numpy as jnp
from jax import lax
from jax.experimental import pallas as pl
from jax.experimental.pallas import tpu as pltpu
from jax.sharding import PartitionSpec as P

ROWS_DEV = 4
OPACITY = 12.0
MESH = pl.DeviceIdType.MESH
F32 = jnp.float32
BF16 = jnp.bfloat16


def kernel(
    n_rx, n_ry, cap, layers, width,
    melt_ref, temp_ref, names_ref, out_ref,
    held, t_ref, send, recv, before, after, lines,
    rhs_b, rhs_d, rhs_e, rhs_p, rhs_n, weights,
    sm, st, gy, gx, img, cin, send2, parts,
    a_send, a_recv, hp_send, hp_recv, hn_send, hn_recv, t_send, t_recv,
    c_send, c_recv, d_send, d_recv, in_sem,
):
    n_dev = n_rx * n_ry
    rows = ROWS_DEV * n_dev
    half_rows = rows // 2
    n_low = n_dev // 2
    k0 = n_ry * 2 * cap
    r, j = lax.axis_index("rx"), lax.axis_index("ry")
    me = r * n_ry + j
    core = r % 2

    def worker(rr, dd):
        return ((rr // 2) * 2 + dd % 2, (dd // 2) * 2 + rr % 2)

    def worker_of(slab):
        return worker(slab // n_ry, slab % n_ry)

    src_r, slab_d = worker(r, j)
    slab = src_r * n_ry + slab_d
    own_block = core == j % 2
    has_prev, has_next = slab > 0, slab < n_dev - 1

    barrier = pltpu.get_barrier_semaphore()

    def greet(i, c):
        other = (me + i) % n_dev
        pl.semaphore_signal(barrier, inc=1, device_id=(other // n_ry, other % n_ry), device_id_type=MESH)
        return c

    lax.fori_loop(1, n_dev, greet, 0)

    loads = [pltpu.make_async_copy(ref, held.at[i], in_sem.at[i]) for i, ref in enumerate((melt_ref, temp_ref))]
    for load in loads:
        load.start()

    lane8 = lax.broadcasted_iota(jnp.int32, (cap, 2 * k0), 1)
    row8 = lax.broadcasted_iota(jnp.int32, (cap, 2 * k0), 0)
    slot = (lane8 // (2 * cap)) & (n_ry - 1)
    named = names_ref[...].astype(F32)
    spread = jnp.zeros((cap, 2 * k0), F32)
    for jj in range(n_ry):
        spread = jnp.where(slot == (j + n_ry - jj) % n_ry, named[:, jj : jj + 1], spread)
    line = jnp.sum(jnp.where(row8 == (lane8 & (cap - 1)), spread, 0.0), axis=0, keepdims=True)
    line = jnp.where(line >= rows, 1e4, line)
    t_ref[...] = jnp.broadcast_to(line, (8, 2 * k0))

    for field in range(2):
        loads[field].wait()
        for d in range(n_ry):
            send[d * layers : (d + 1) * layers, field * cap : (field + 1) * cap, :] = (
                held[field, :, d * cap : (d + 1) * cap, :])

    before[:, 0, cap : 2 * cap, :] = jnp.zeros((n_ry, cap, width), F32)
    after[:, 1, cap : 2 * cap, :] = jnp.zeros((n_ry, cap, width), F32)

    @pl.when(jnp.logical_not(has_prev))
    def _():
        before[...] = jnp.zeros_like(before)
        lines[1] = jnp.full_like(lines[1], 1e4)

    @pl.when(jnp.logical_not(has_next))
    def _():
        after[...] = jnp.zeros_like(after)
        lines[2] = jnp.full_like(lines[2], 1e4)

    pl.semaphore_wait(barrier, n_dev - 1)

    def line_copy(which, target):
        return pltpu.make_async_remote_copy(
            t_ref, lines.at[which], t_send.at[which], t_recv.at[which],
            device_id=target, device_id_type=MESH)

    @pl.when(me < n_dev - 1)
    def _():
        line_copy(1, worker_of(me + 1)).start()

    @pl.when(me > 0)
    def _():
        line_copy(2, worker_of(me - 1)).start()

    @pl.when(own_block)
    def _():
        lines[0] = t_ref[...]

    @pl.when(jnp.logical_not(own_block))
    def _():
        line_copy(0, worker(r, j)).start()

    def brick_copy(i):
        d = (j + i) % n_ry
        return pltpu.make_async_remote_copy(
            send.at[pl.ds(d * layers, layers)], recv.at[i], a_send.at[i], a_recv.at[i],
            device_id=worker(r, d), device_id_type=MESH)

    for i in range(1, n_ry):
        brick_copy(i).start()

    @pl.when(jnp.logical_not(own_block))
    def _():
        brick_copy(0).start()

    @pl.when(own_block)
    def _():
        recv[0] = send[pl.ds(j * layers, layers)]

    @pl.when(jnp.logical_not(own_block))
    def _():
        line_copy(0, worker(r, j)).wait_recv()

    @pl.when(has_prev)
    def _():
        line_copy(1, worker(r, j)).wait_recv()

    @pl.when(has_next)
    def _():
        line_copy(2, worker(r, j)).wait_recv()

    p = lax.broadcasted_iota(jnp.int32, (rows, 2 * k0), 0)
    lane = lax.broadcasted_iota(jnp.int32, (rows, 2 * k0), 1)
    log_ry, log_low = n_ry.bit_length() - 1, n_low.bit_length() - 1
    other_half = jnp.where(p < half_rows, 1, 0)
    side = jnp.where(other_half == 1, 1 - core, core)
    part_a = (p >> log_low) & (ROWS_DEV - 1)
    low = p & (n_low - 1)
    k = ((low >> log_ry) << (log_ry + 1)) + side * n_ry + (low & (n_ry - 1))
    q = (part_a * n_dev + k).astype(F32)
    is_melt = (lane & cap) == 0

    def hat(v):
        return jnp.maximum(0.5 - 0.25 * jnp.abs(v), 0.0)

    for which in range(3):
        u = lines[which, 0:1, :] - q
        s = hat(u)
        g = 0.5 * (jnp.where(q < rows - 1, hat(u - 1.0), 0.0) - jnp.where(q > 0, hat(u + 1.0), 0.0))
        weights[which, 0:rows] = jnp.where(is_melt, s, 0.0).astype(BF16)
        weights[which, rows : 2 * rows] = jnp.where(is_melt, 0.0, s).astype(BF16)
        weights[which, 2 * rows : 3 * rows] = jnp.where(is_melt, g, 0.0).astype(BF16)

    col = lax.broadcasted_iota(jnp.int32, (4 * cap, width), 1)

    def from_left(x):
        return jnp.where(col == 0, 0.0, pltpu.roll(x, 1, 1))

    def from_right(x):
        return jnp.where(col == width - 1, 0.0, pltpu.roll(x, width - 1, 1))

    def smooth_x(x):
        return 0.5 * x + 0.25 * (from_left(x) + from_right(x))

    def diff_x(x):
        return 0.5 * (from_right(x) - from_left(x))

    def put(ref, index, first, x):
        hi = x.astype(BF16)
        ref[index, first : first + 4 * cap] = hi
        ref[index, k0 + first : k0 + first + 4 * cap] = (x - hi.astype(F32)).astype(BF16)

    def rows_of(ref, pair, layer):
        return ref[2 * pair : 2 * pair + 2, layer].reshape(4 * cap, width)

    class Both:
        def __init__(self, copies):
            self.start = lambda: [c.start() for c in copies]
            self.wait_recv = lambda: [c.wait_recv() for c in copies]
            self.wait_send = lambda: [c.wait_send() for c in copies]

    def halo(jj, ref, near, far, near_at, far_at, sends, recvs, target):
        return Both([
            pltpu.make_async_remote_copy(
                recv.at[jj, near], ref.at[jj, near_at], sends.at[0, jj], recvs.at[0, jj],
                device_id=target, device_id_type=MESH),
            pltpu.make_async_remote_copy(
                recv.at[jj, far, pl.ds(0, cap)], ref.at[jj, far_at, pl.ds(0, cap)], sends.at[1, jj], recvs.at[1, jj],
                device_id=target, device_id_type=MESH),
        ])

    def before_copy(jj):
        return halo(jj, before, layers - 1, layers - 2, 1, 0, hp_send, hp_recv, worker_of((slab + 1) % n_dev))

    def after_copy(jj):
        return halo(jj, after, 0, 1, 0, 1, hn_send, hn_recv, worker_of((slab + n_dev - 1) % n_dev))

    def brick_wait(jj):
        pltpu.make_async_remote_copy(
            send.at[pl.ds(0, layers)], recv.at[jj], a_send.at[0], a_recv.at[jj],
            device_id=worker(r, j), device_id_type=MESH).wait_recv()

    for pair in range(n_ry // 2):
        for jj in (2 * pair, 2 * pair + 1):
            if jj:
                brick_wait(jj)
            else:
                @pl.when(jnp.logical_not(own_block))
                def _():
                    brick_wait(0)

            @pl.when(has_next)
            def _():
                before_copy(jj).start()

            @pl.when(has_prev)
            def _():
                after_copy(jj).start()

        first = pair * 4 * cap
        xs = [smooth_x(rows_of(recv, pair, z)) for z in range(layers)]
        for z in range(layers):
            b = 0.5 * xs[z]
            if z > 0:
                b = b + 0.25 * xs[z - 1]
            if z < layers - 1:
                b = b + 0.25 * xs[z + 1]
            put(rhs_b, z, first, b)
            put(rhs_d, z, first, diff_x(b))
        put(rhs_e, 0, first, 0.25 * xs[0])
        put(rhs_e, 1, first, 0.25 * xs[layers - 1])

    def dot(which, lo, hi, rhs):
        return jnp.dot(weights[which, lo * rows : hi * rows], rhs, preferred_element_type=F32)

    for z in range(layers):
        res = dot(0, 0, 3, rhs_b[z])
        sm[z + 1] = res[0:rows]
        st[z] = res[rows : 2 * rows]
        gy[z] = res[2 * rows : 3 * rows]
        gx[z] = dot(0, 0, 1, rhs_d[z])
    sm[0] = dot(0, 0, 1, rhs_e[0])
    sm[layers + 1] = dot(0, 0, 1, rhs_e[1])

    for pair in range(n_ry // 2):
        for jj in (2 * pair, 2 * pair + 1):
            @pl.when(has_prev)
            def _():
                before_copy(jj).wait_recv()

            @pl.when(has_next)
            def _():
                after_copy(jj).wait_recv()

        first = pair * 4 * cap
        p3, p4 = (smooth_x(rows_of(before, pair, z)) for z in (0, 1))
        n0, n1 = (smooth_x(rows_of(after, pair, z)) for z in (0, 1))
        put(rhs_p, 0, first, 0.25 * p4)
        put(rhs_p, 1, first, 0.25 * diff_x(p4))
        put(rhs_p, 2, first, 0.25 * p3 + 0.5 * p4)
        put(rhs_n, 0, first, 0.25 * n0)
        put(rhs_n, 1, first, 0.25 * diff_x(n0))
        put(rhs_n, 2, first, 0.25 * n1 + 0.5 * n0)

    for which, rhs, z, edge, present in ((1, rhs_p, 0, 0, has_prev), (2, rhs_n, layers - 1, layers + 1, has_next)):
        res = dot(which, 0, 3, rhs[0])
        sm[z + 1] += res[0:rows]
        st[z] += res[rows : 2 * rows]
        gy[z] += res[2 * rows : 3 * rows]
        gx[z] += dot(which, 0, 1, rhs[1])
        sm[edge] = jnp.where(present, sm[edge] + dot(which, 0, 1, rhs[2]), 0.0)

    decay = -OPACITY / (layers * n_dev)

    quarter = half_rows // 2

    def march(half, part):
        def tile(i, c):
            at = pl.ds(pl.multiple_of(half * half_rows + part * quarter + i * 8, 8), 8)
            through = total = red = green = None
            for z in range(layers):
                s = sm[z + 1, at, :]
                dz = 0.5 * (sm[z + 2, at, :] - sm[z, at, :])
                dy, dx = gy[z, at, :], gx[z, at, :]
                t = st[z, at, :]
                facing = (0.48 * dz + 0.6 * dy + 0.64 * dx) * lax.rsqrt(dz * dz + dy * dy + dx * dx + 0.01)
                shade = 0.3 + 0.7 * jnp.abs(facing)
                kept = jnp.exp(s * decay)
                w = (1.0 - kept) * shade
                if z > 0:
                    w = w * through
                rw = w / (1.0 + jnp.exp(-2.0 * t))
                gw = w * jnp.exp(-t * t)
                if z == 0:
                    through, total, red, green = kept, w, rw, gw
                else:
                    through, total, red, green = through * kept, total + w, red + rw, green + gw
            to = pl.ds(pl.multiple_of(i * 8, 8), 8)
            img[half, part, 0, to, :] = red
            img[half, part, 1, to, :] = green
            img[half, part, 2, to, :] = total - red
            img[half, part, 3, to, :] = through
            return c

        lax.fori_loop(0, quarter // 8, tile, 0)

    def core_copy(part):
        return pltpu.make_async_remote_copy(
            img.at[0, part], cin.at[part], c_send.at[part], c_recv.at[part],
            device_id=((r // 2) * 2 + 1 - core, j), device_id_type=MESH)

    front = core == 0
    low_me = (r // 2) * n_ry + j
    group = (r // 2) * n_ry + (j % 2) * (n_ry // 2) + j // 2

    def part_copy(part, i):
        to = (low_me + i) % n_low
        return pltpu.make_async_remote_copy(
            send2.at[part, to], parts.at[part, group], d_send.at[part, i], d_recv.at[part, group],
            device_id=((to // n_ry) * 2 + core, to % n_ry), device_id_type=MESH)

    for part in range(2):
        march(0, part)
        core_copy(part).start()
        march(1, part)
        core_copy(part).wait_recv()
        for a in range(2):
            for low8 in range(n_low // 8):
                at = slice(a * n_low + low8 * 8, a * n_low + low8 * 8 + 8)
                mine = [img[1, part, ch, at, :] for ch in range(4)]
                theirs = [cin[part, ch, at, :] for ch in range(4)]
                ft = jnp.where(front, mine[3], theirs[3])
                for ch in range(4):
                    f = jnp.where(front, mine[ch], theirs[ch])
                    b = jnp.where(front, theirs[ch], mine[ch])
                    value = f + ft * b if ch < 3 else ft * b
                    send2[part, low8 * 8 : low8 * 8 + 8, ch * 2 + a, :] = value
        for i in range(1, n_low):
            part_copy(part, i).start()
        parts[part, group] = send2[part, low_me]

    for part in range(2):
        color, through = None, None
        for g in range(n_low):
            @pl.when(g != group)
            def _():
                pltpu.make_async_remote_copy(
                    send2.at[part, 0], parts.at[part, g], d_send.at[part, 0], d_recv.at[part, g],
                    device_id=(r, j), device_id_type=MESH).wait_recv()

            value = parts[part, g]
            t = jnp.concatenate([value[6:8]] * 4, axis=0)
            if g == 0:
                color, through = value, t
            else:
                color = color + through * value
                through = through * t
        for a in range(2):
            for ch in range(4):
                at = ch * 2 + a
                out_ref[ch, part * 2 + a] = (color if ch < 3 else through)[at : at + 1]

    @pl.when(me < n_dev - 1)
    def _():
        line_copy(1, worker(r, j)).wait_send()

    @pl.when(me > 0)
    def _():
        line_copy(2, worker(r, j)).wait_send()

    @pl.when(jnp.logical_not(own_block))
    def _():
        line_copy(0, worker(r, j)).wait_send()
        brick_copy(0).wait_send()

    for i in range(1, n_ry):
        brick_copy(i).wait_send()
    for jj in range(n_ry):
        @pl.when(has_next)
        def _():
            before_copy(jj).wait_send()

        @pl.when(has_prev)
        def _():
            after_copy(jj).wait_send()

    for part in range(2):
        core_copy(part).wait_send()
        for i in range(1, n_low):
            part_copy(part, i).wait_send()


def shards(liquid_share, thermal_field, destination_slab_line):
    n_rx, n_ry = lax.axis_size("rx"), lax.axis_size("ry")
    bricks, layers, width = liquid_share.shape
    cap = bricks // n_ry
    n_dev = n_rx * n_ry
    rows = ROWS_DEV * n_dev
    k0 = n_ry * 2 * cap
    dma = pltpu.SemaphoreType.DMA
    vmem = pltpu.VMEM
    half_rows, n_low = rows // 2, n_dev // 2
    image = pl.pallas_call(
        functools.partial(kernel, n_rx, n_ry, cap, layers, width),
        out_shape=jax.ShapeDtypeStruct((4, ROWS_DEV, 1, width), F32),
        in_specs=[pl.BlockSpec(memory_space=pl.ANY)] * 2 + [pl.BlockSpec(memory_space=pltpu.VMEM)],
        out_specs=pl.BlockSpec(memory_space=pltpu.VMEM),
        scratch_shapes=[
            vmem((2, layers, bricks, width), F32),
            vmem((8, 2 * k0), F32),
            vmem((n_ry * layers, 2 * cap, width), F32),
            vmem((n_ry, layers, 2 * cap, width), F32),
            vmem((n_ry, 2, 2 * cap, width), F32),
            vmem((n_ry, 2, 2 * cap, width), F32),
            vmem((3, 8, 2 * k0), F32),
            vmem((layers, 2 * k0, width), BF16),
            vmem((layers, 2 * k0, width), BF16),
            vmem((2, 2 * k0, width), BF16),
            vmem((3, 2 * k0, width), BF16),
            vmem((3, 2 * k0, width), BF16),
            vmem((3, 3 * rows, 2 * k0), BF16),
            vmem((layers + 2, rows, width), F32),
            vmem((layers, rows, width), F32),
            vmem((layers, rows, width), F32),
            vmem((layers, rows, width), F32),
            vmem((2, 2, 4, half_rows // 2, width), F32),
            vmem((2, 4, half_rows // 2, width), F32),
            vmem((2, n_low, 2 * ROWS_DEV, width), F32),
            vmem((2, n_low, 2 * ROWS_DEV, width), F32),
            dma((n_ry,)), dma((n_ry,)),
            dma((2, n_ry)), dma((2, n_ry)),
            dma((2, n_ry)), dma((2, n_ry)),
            dma((3,)), dma((3,)),
            dma((2,)), dma((2,)),
            dma((2, n_low)), dma((2, n_low)),
            dma((2,)),
        ],
        compiler_params=pltpu.CompilerParams(
            collective_id=0, has_side_effects=True, vmem_limit_bytes=60 * 1024 * 1024),
    )(
        jnp.transpose(liquid_share, (1, 0, 2)),
        jnp.transpose(thermal_field, (1, 0, 2)),
        jnp.transpose(destination_slab_line[0]),
    )
    return image


def solution(mesh):
    return jax.shard_map(
        shards,
        mesh=mesh,
        in_specs=(
            P(("rx", "ry"), None, None),
            P(("rx", "ry"), None, None),
            P(("rx", "ry"), None, None),
        ),
        out_specs=P(None, None, ("rx", "ry"), None),
        check_vma=False,
    )
```

```python
import functools

import jax
import jax.numpy as jnp
from jax import lax
from jax.experimental import pallas as pl
from jax.experimental.pallas import tpu as pltpu
from jax.sharding import PartitionSpec as P

ROWS_DEV = 4
OPACITY = 12.0
MESH = pl.DeviceIdType.MESH
F32 = jnp.float32
BF16 = jnp.bfloat16


def kernel(
    n_rx, n_ry, cap, layers, width,
    melt_ref, temp_ref, names_ref, out_ref,
    held, t_ref, send, recv, before, after, lines,
    rhs_b, rhs_d, rhs_e, rhs_p, rhs_n, weights,
    sm, st, gy, gx, img, cin, img2, cin2, send2, parts,
    a_send, a_recv, hp_send, hp_recv, hn_send, hn_recv, t_send, t_recv,
    c_send, c_recv, d_send, d_recv, e_send, e_recv, in_sem,
):
    n_dev = n_rx * n_ry
    rows = ROWS_DEV * n_dev
    half_rows = rows // 2
    n_low = n_dev // 2
    k0 = n_ry * 2 * cap
    r, j = lax.axis_index("rx"), lax.axis_index("ry")
    me = r * n_ry + j
    core = r % 2
    bit1 = (j // 2) % 2
    n_rest = n_low // 2

    def worker(rr, dd):
        return ((rr // 2) * 2 + dd % 2, (dd // 2) * 2 + rr % 2)

    def worker_of(slab):
        return worker(slab // n_ry, slab % n_ry)

    src_r, slab_d = worker(r, j)
    slab = src_r * n_ry + slab_d
    own_block = core == j % 2
    has_prev, has_next = slab > 0, slab < n_dev - 1

    barrier = pltpu.get_barrier_semaphore()

    def greet(i, c):
        other = (me + i) % n_dev
        pl.semaphore_signal(barrier, inc=1, device_id=(other // n_ry, other % n_ry), device_id_type=MESH)
        return c

    lax.fori_loop(1, n_dev, greet, 0)

    loads = [pltpu.make_async_copy(ref, held.at[i], in_sem.at[i]) for i, ref in enumerate((melt_ref, temp_ref))]
    for load in loads:
        load.start()

    lane8 = lax.broadcasted_iota(jnp.int32, (cap, 2 * k0), 1)
    row8 = lax.broadcasted_iota(jnp.int32, (cap, 2 * k0), 0)
    slot = (lane8 // (2 * cap)) & (n_ry - 1)
    named = names_ref[...].astype(F32)
    spread = jnp.zeros((cap, 2 * k0), F32)
    for jj in range(n_ry):
        spread = jnp.where(slot == (j + n_ry - jj) % n_ry, named[:, jj : jj + 1], spread)
    line = jnp.sum(jnp.where(row8 == (lane8 & (cap - 1)), spread, 0.0), axis=0, keepdims=True)
    line = jnp.where(line >= rows, 1e4, line)
    t_ref[...] = jnp.broadcast_to(line, (8, 2 * k0))

    for field in range(2):
        loads[field].wait()
        for d in range(n_ry):
            send[d * layers : (d + 1) * layers, field * cap : (field + 1) * cap, :] = (
                held[field, :, d * cap : (d + 1) * cap, :])

    before[:, 0, cap : 2 * cap, :] = jnp.zeros((n_ry, cap, width), F32)
    after[:, 1, cap : 2 * cap, :] = jnp.zeros((n_ry, cap, width), F32)

    @pl.when(jnp.logical_not(has_prev))
    def _():
        before[...] = jnp.zeros_like(before)
        lines[1] = jnp.full_like(lines[1], 1e4)

    @pl.when(jnp.logical_not(has_next))
    def _():
        after[...] = jnp.zeros_like(after)
        lines[2] = jnp.full_like(lines[2], 1e4)

    pl.semaphore_wait(barrier, n_dev - 1)

    def line_copy(which, target):
        return pltpu.make_async_remote_copy(
            t_ref, lines.at[which], t_send.at[which], t_recv.at[which],
            device_id=target, device_id_type=MESH)

    @pl.when(me < n_dev - 1)
    def _():
        line_copy(1, worker_of(me + 1)).start()

    @pl.when(me > 0)
    def _():
        line_copy(2, worker_of(me - 1)).start()

    @pl.when(own_block)
    def _():
        lines[0] = t_ref[...]

    @pl.when(jnp.logical_not(own_block))
    def _():
        line_copy(0, worker(r, j)).start()

    def brick_copy(i):
        d = (j + i) % n_ry
        return pltpu.make_async_remote_copy(
            send.at[pl.ds(d * layers, layers)], recv.at[i], a_send.at[i], a_recv.at[i],
            device_id=worker(r, d), device_id_type=MESH)

    for i in range(1, n_ry):
        brick_copy(i).start()

    @pl.when(jnp.logical_not(own_block))
    def _():
        brick_copy(0).start()

    @pl.when(own_block)
    def _():
        recv[0] = send[pl.ds(j * layers, layers)]

    @pl.when(jnp.logical_not(own_block))
    def _():
        line_copy(0, worker(r, j)).wait_recv()

    @pl.when(has_prev)
    def _():
        line_copy(1, worker(r, j)).wait_recv()

    @pl.when(has_next)
    def _():
        line_copy(2, worker(r, j)).wait_recv()

    p = lax.broadcasted_iota(jnp.int32, (rows, 2 * k0), 0)
    lane = lax.broadcasted_iota(jnp.int32, (rows, 2 * k0), 1)
    log_ry, log_low = n_ry.bit_length() - 1, n_low.bit_length() - 1
    other_half = jnp.where(p < half_rows, 1, 0)
    side = jnp.where(other_half == 1, 1 - core, core)
    log_rest = log_low - 1
    rest = p & (n_rest - 1)
    part_a = ((p >> (log_rest + 2)) & 1) * 2 + ((p >> log_rest) & 1)
    side2 = jnp.where(((p >> (log_rest + 1)) & 1) == 0, 1 - bit1, bit1)
    j_low = rest & (n_ry // 2 - 1)
    k_j = ((j_low >> 1) << 2) + side2 * 2 + (j_low & 1)
    k = ((rest >> (log_ry - 1)) << (log_ry + 1)) + side * n_ry + k_j
    q = (part_a * n_dev + k).astype(F32)
    is_melt = (lane & cap) == 0

    def hat(v):
        return jnp.maximum(0.5 - 0.25 * jnp.abs(v), 0.0)

    for which in range(3):
        u = lines[which, 0:1, :] - q
        s = hat(u)
        g = 0.5 * (jnp.where(q < rows - 1, hat(u - 1.0), 0.0) - jnp.where(q > 0, hat(u + 1.0), 0.0))
        weights[which, 0:rows] = jnp.where(is_melt, s, 0.0).astype(BF16)
        weights[which, rows : 2 * rows] = jnp.where(is_melt, 0.0, s).astype(BF16)
        weights[which, 2 * rows : 3 * rows] = jnp.where(is_melt, g, 0.0).astype(BF16)

    col = lax.broadcasted_iota(jnp.int32, (4 * cap, width), 1)

    def from_left(x):
        return jnp.where(col == 0, 0.0, pltpu.roll(x, 1, 1))

    def from_right(x):
        return jnp.where(col == width - 1, 0.0, pltpu.roll(x, width - 1, 1))

    def smooth_x(x):
        return 0.5 * x + 0.25 * (from_left(x) + from_right(x))

    def diff_x(x):
        return 0.5 * (from_right(x) - from_left(x))

    def put(ref, index, first, x):
        hi = x.astype(BF16)
        ref[index, first : first + 4 * cap] = hi
        ref[index, k0 + first : k0 + first + 4 * cap] = (x - hi.astype(F32)).astype(BF16)

    def rows_of(ref, pair, layer):
        return ref[2 * pair : 2 * pair + 2, layer].reshape(4 * cap, width)

    class Both:
        def __init__(self, copies):
            self.start = lambda: [c.start() for c in copies]
            self.wait_recv = lambda: [c.wait_recv() for c in copies]
            self.wait_send = lambda: [c.wait_send() for c in copies]

    def halo(jj, ref, near, far, near_at, far_at, sends, recvs, target):
        return Both([
            pltpu.make_async_remote_copy(
                recv.at[jj, near], ref.at[jj, near_at], sends.at[0, jj], recvs.at[0, jj],
                device_id=target, device_id_type=MESH),
            pltpu.make_async_remote_copy(
                recv.at[jj, far, pl.ds(0, cap)], ref.at[jj, far_at, pl.ds(0, cap)], sends.at[1, jj], recvs.at[1, jj],
                device_id=target, device_id_type=MESH),
        ])

    def before_copy(jj):
        return halo(jj, before, layers - 1, layers - 2, 1, 0, hp_send, hp_recv, worker_of((slab + 1) % n_dev))

    def after_copy(jj):
        return halo(jj, after, 0, 1, 0, 1, hn_send, hn_recv, worker_of((slab + n_dev - 1) % n_dev))

    def brick_wait(jj):
        pltpu.make_async_remote_copy(
            send.at[pl.ds(0, layers)], recv.at[jj], a_send.at[0], a_recv.at[jj],
            device_id=worker(r, j), device_id_type=MESH).wait_recv()

    for pair in range(n_ry // 2):
        for jj in (2 * pair, 2 * pair + 1):
            if jj:
                brick_wait(jj)
            else:
                @pl.when(jnp.logical_not(own_block))
                def _():
                    brick_wait(0)

            @pl.when(has_next)
            def _():
                before_copy(jj).start()

            @pl.when(has_prev)
            def _():
                after_copy(jj).start()

        first = pair * 4 * cap
        xs = [smooth_x(rows_of(recv, pair, z)) for z in range(layers)]
        for z in range(layers):
            b = 0.5 * xs[z]
            if z > 0:
                b = b + 0.25 * xs[z - 1]
            if z < layers - 1:
                b = b + 0.25 * xs[z + 1]
            put(rhs_b, z, first, b)
            put(rhs_d, z, first, diff_x(b))
        put(rhs_e, 0, first, 0.25 * xs[0])
        put(rhs_e, 1, first, 0.25 * xs[layers - 1])

    def dot(which, lo, hi, rhs):
        return jnp.dot(weights[which, lo * rows : hi * rows], rhs, preferred_element_type=F32)

    for z in range(layers):
        res = dot(0, 0, 3, rhs_b[z])
        sm[z + 1] = res[0:rows]
        st[z] = res[rows : 2 * rows]
        gy[z] = res[2 * rows : 3 * rows]
        gx[z] = dot(0, 0, 1, rhs_d[z])
    sm[0] = dot(0, 0, 1, rhs_e[0])
    sm[layers + 1] = dot(0, 0, 1, rhs_e[1])

    for pair in range(n_ry // 2):
        for jj in (2 * pair, 2 * pair + 1):
            @pl.when(has_prev)
            def _():
                before_copy(jj).wait_recv()

            @pl.when(has_next)
            def _():
                after_copy(jj).wait_recv()

        first = pair * 4 * cap
        p3, p4 = (smooth_x(rows_of(before, pair, z)) for z in (0, 1))
        n0, n1 = (smooth_x(rows_of(after, pair, z)) for z in (0, 1))
        put(rhs_p, 0, first, 0.25 * p4)
        put(rhs_p, 1, first, 0.25 * diff_x(p4))
        put(rhs_p, 2, first, 0.25 * p3 + 0.5 * p4)
        put(rhs_n, 0, first, 0.25 * n0)
        put(rhs_n, 1, first, 0.25 * diff_x(n0))
        put(rhs_n, 2, first, 0.25 * n1 + 0.5 * n0)

    for which, rhs, z, edge, present in ((1, rhs_p, 0, 0, has_prev), (2, rhs_n, layers - 1, layers + 1, has_next)):
        res = dot(which, 0, 3, rhs[0])
        sm[z + 1] += res[0:rows]
        st[z] += res[rows : 2 * rows]
        gy[z] += res[2 * rows : 3 * rows]
        gx[z] += dot(which, 0, 1, rhs[1])
        sm[edge] = jnp.where(present, sm[edge] + dot(which, 0, 1, rhs[2]), 0.0)

    decay = -OPACITY / (layers * n_dev)

    quarter = half_rows // 2

    def march(half, part):
        def tile(i, c):
            at = pl.ds(pl.multiple_of(half * half_rows + part * quarter + i * 8, 8), 8)
            through = total = red = green = None
            for z in range(layers):
                s = sm[z + 1, at, :]
                dz = 0.5 * (sm[z + 2, at, :] - sm[z, at, :])
                dy, dx = gy[z, at, :], gx[z, at, :]
                t = st[z, at, :]
                facing = (0.48 * dz + 0.6 * dy + 0.64 * dx) * lax.rsqrt(dz * dz + dy * dy + dx * dx + 0.01)
                shade = 0.3 + 0.7 * jnp.abs(facing)
                kept = jnp.exp(s * decay)
                w = (1.0 - kept) * shade
                if z > 0:
                    w = w * through
                rw = w / (1.0 + jnp.exp(-2.0 * t))
                gw = w * jnp.exp(-t * t)
                if z == 0:
                    through, total, red, green = kept, w, rw, gw
                else:
                    through, total, red, green = through * kept, total + w, red + rw, green + gw
            to = pl.ds(pl.multiple_of(i * 8, 8), 8)
            img[half, part, 0, to, :] = red
            img[half, part, 1, to, :] = green
            img[half, part, 2, to, :] = total - red
            img[half, part, 3, to, :] = through
            return c

        lax.fori_loop(0, quarter // 8, tile, 0)

    def core_copy(part):
        return pltpu.make_async_remote_copy(
            img.at[0, part], cin.at[part], c_send.at[part], c_recv.at[part],
            device_id=((r // 2) * 2 + 1 - core, j), device_id_type=MESH)

    rest_me = (r // 2) * (n_ry // 2) + (j // 4) * 2 + j % 2
    group = (r // 2) * (n_ry // 2) + (j % 2) * (n_ry // 4) + j // 4

    def chip_copy(part):
        return pltpu.make_async_remote_copy(
            img2.at[part, 0], cin2.at[part], e_send.at[part], e_recv.at[part],
            device_id=(r, j + 2 - 4 * bit1), device_id_type=MESH)

    def part_copy(part, i):
        to = (rest_me + i) % n_rest
        to_j = to % (n_ry // 2)
        return pltpu.make_async_remote_copy(
            send2.at[part, to], parts.at[part, group], d_send.at[part, i], d_recv.at[part, group],
            device_id=((to // (n_ry // 2)) * 2 + core, (to_j // 2) * 4 + bit1 * 2 + to_j % 2), device_id_type=MESH)

    def over(front, mine, theirs):
        ft = jnp.where(front, mine[3], theirs[3])
        for ch in range(4):
            f = jnp.where(front, mine[ch], theirs[ch])
            b = jnp.where(front, theirs[ch], mine[ch])
            yield f + ft * b if ch < 3 else ft * b

    def finish_core(part):
        core_copy(part).wait_recv()
        for h in range(2):
            for first in range(0, n_low, 8):
                at = slice(h * n_low + first, h * n_low + first + 8)
                mine = [img[1, part, ch, at, :] for ch in range(4)]
                theirs = [cin[part, ch, at, :] for ch in range(4)]
                for ch, value in enumerate(over(core == 0, mine, theirs)):
                    img2[part, h, ch, first : first + 8, :] = value
        chip_copy(part).start()

    def finish_chip(part):
        chip_copy(part).wait_recv()
        for a in range(2):
            for first in range(0, n_rest, 8):
                at = slice(a * n_rest + first, a * n_rest + first + 8)
                mine = [img2[part, 1, ch, at, :] for ch in range(4)]
                theirs = [cin2[part, ch, at, :] for ch in range(4)]
                for ch, value in enumerate(over(bit1 == 0, mine, theirs)):
                    send2[part, first : first + 8, ch * 2 + a, :] = value
        for i in range(1, n_rest):
            part_copy(part, i).start()
        parts[part, group] = send2[part, rest_me]

    march(0, 0)
    core_copy(0).start()
    march(1, 0)
    finish_core(0)
    march(0, 1)
    core_copy(1).start()
    march(1, 1)
    finish_core(1)
    finish_chip(0)
    finish_chip(1)

    for part in range(2):
        color, through = None, None
        for g in range(n_rest):
            @pl.when(g != group)
            def _():
                pltpu.make_async_remote_copy(
                    send2.at[part, 0], parts.at[part, g], d_send.at[part, 0], d_recv.at[part, g],
                    device_id=(r, j), device_id_type=MESH).wait_recv()

            value = parts[part, g]
            t = jnp.concatenate([value[6:8]] * 4, axis=0)
            if g == 0:
                color, through = value, t
            else:
                color = color + through * value
                through = through * t
        for a in range(2):
            for ch in range(4):
                at = ch * 2 + a
                out_ref[ch, part * 2 + a] = (color if ch < 3 else through)[at : at + 1]

    @pl.when(me < n_dev - 1)
    def _():
        line_copy(1, worker(r, j)).wait_send()

    @pl.when(me > 0)
    def _():
        line_copy(2, worker(r, j)).wait_send()

    @pl.when(jnp.logical_not(own_block))
    def _():
        line_copy(0, worker(r, j)).wait_send()
        brick_copy(0).wait_send()

    for i in range(1, n_ry):
        brick_copy(i).wait_send()
    for jj in range(n_ry):
        @pl.when(has_next)
        def _():
            before_copy(jj).wait_send()

        @pl.when(has_prev)
        def _():
            after_copy(jj).wait_send()

    for part in range(2):
        core_copy(part).wait_send()
        chip_copy(part).wait_send()
        for i in range(1, n_rest):
            part_copy(part, i).wait_send()


def shards(liquid_share, thermal_field, destination_slab_line):
    n_rx, n_ry = lax.axis_size("rx"), lax.axis_size("ry")
    bricks, layers, width = liquid_share.shape
    cap = bricks // n_ry
    n_dev = n_rx * n_ry
    rows = ROWS_DEV * n_dev
    k0 = n_ry * 2 * cap
    dma = pltpu.SemaphoreType.DMA
    vmem = pltpu.VMEM
    half_rows, n_low = rows // 2, n_dev // 2
    image = pl.pallas_call(
        functools.partial(kernel, n_rx, n_ry, cap, layers, width),
        out_shape=jax.ShapeDtypeStruct((4, ROWS_DEV, 1, width), F32),
        in_specs=[pl.BlockSpec(memory_space=pl.ANY)] * 2 + [pl.BlockSpec(memory_space=pltpu.VMEM)],
        out_specs=pl.BlockSpec(memory_space=pltpu.VMEM),
        scratch_shapes=[
            vmem((2, layers, bricks, width), F32),
            vmem((8, 2 * k0), F32),
            vmem((n_ry * layers, 2 * cap, width), F32),
            vmem((n_ry, layers, 2 * cap, width), F32),
            vmem((n_ry, 2, 2 * cap, width), F32),
            vmem((n_ry, 2, 2 * cap, width), F32),
            vmem((3, 8, 2 * k0), F32),
            vmem((layers, 2 * k0, width), BF16),
            vmem((layers, 2 * k0, width), BF16),
            vmem((2, 2 * k0, width), BF16),
            vmem((3, 2 * k0, width), BF16),
            vmem((3, 2 * k0, width), BF16),
            vmem((3, 3 * rows, 2 * k0), BF16),
            vmem((layers + 2, rows, width), F32),
            vmem((layers, rows, width), F32),
            vmem((layers, rows, width), F32),
            vmem((layers, rows, width), F32),
            vmem((2, 2, 4, half_rows // 2, width), F32),
            vmem((2, 4, half_rows // 2, width), F32),
            vmem((2, 2, 4, half_rows // 4, width), F32),
            vmem((2, 4, half_rows // 4, width), F32),
            vmem((2, n_low // 2, 2 * ROWS_DEV, width), F32),
            vmem((2, n_low // 2, 2 * ROWS_DEV, width), F32),
            dma((n_ry,)), dma((n_ry,)),
            dma((2, n_ry)), dma((2, n_ry)),
            dma((2, n_ry)), dma((2, n_ry)),
            dma((3,)), dma((3,)),
            dma((2,)), dma((2,)),
            dma((2, n_low)), dma((2, n_low)),
            dma((2,)), dma((2,)),
            dma((2,)),
        ],
        compiler_params=pltpu.CompilerParams(
            collective_id=0, has_side_effects=True, vmem_limit_bytes=60 * 1024 * 1024),
    )(
        jnp.transpose(liquid_share, (1, 0, 2)),
        jnp.transpose(thermal_field, (1, 0, 2)),
        jnp.transpose(destination_slab_line[0]),
    )
    return image


def solution(mesh):
    return jax.shard_map(
        shards,
        mesh=mesh,
        in_specs=(
            P(("rx", "ry"), None, None),
            P(("rx", "ry"), None, None),
            P(("rx", "ry"), None, None),
        ),
        out_specs=P(None, None, ("rx", "ry"), None),
        check_vma=False,
    )
```
